32 devices in a mesh: patch: 4 (over z), dev: 8 (over y, x, core).
Axes of the slice: x: 2, y: 2, z: 4, core: 2. Of those that a mesh axis runs over, the one named last changes fastest.
Arguments:
- measure_plane: float32 [2, 65536], P(None, ('patch', 'dev')), may hold values from -1 to 1
- measure_weight: float32 [65536], P(('patch', 'dev')), may hold values from 0.1 to 2
- measure_visit: int32 [65536], P(('patch', 'dev')), may hold values from 0 to 63
- measure_holder: int32 [65536, 1], P(('patch', 'dev')), may hold values from 0 to 7; in each aligned block of 2048 rows (0 to 2047, 2048 to 4095, ...) at most 640 rows name the same one
- measure_star: int32 [65536], P(('patch', 'dev')), may hold values from 0 to 255
- visit_coefficients: float32 [512, 56], P('dev'), may hold values from -4 to 4
- star_location: float32 [2, 8192], P(None, ('patch', 'dev')), may hold values from -6 to 6
Outputs:
- schur_blocks: float32 [512, 784], P('dev')
- schur_rhs: float32 [512, 56], P('dev')
- star_offset: float32 [2, 8192], P(None, ('patch', 'dev'))
The draws below stay inside these ranges and needn't reach their ends.
Inputs may be any that keep to these rules, and one draw needn't show every extreme that they name: `measure_holder`: in each aligned block of 2048 rows (the rows of one device) no value appears more than 640 times.
All inputs are finite; a program needn't handle non-finite values.
Results may differ from the reference program's by a relative error of at most 0.0001.
Values sent between devices are 32-bit elements; how exact they have to be, the bound alone decides.
A program may use at most 64 MiB of HBM per device.

```python
import math
import jax
import jax.numpy as jnp
import numpy as np
from jax import lax

NMON = 28
MEASURES_LOCAL = 2048
VISITS_LOCAL = 64
STARS_LOCAL = 256
MEASURE_LIMIT = 640
VISITS = 512
TOTAL_STARS = 8192
TOTAL_MEASURES = 65536
N_PATCH = 4
N_DEV = 8


def draw_measure_star(key, part):
    key = jax.random.fold_in(key, 7)
    key_toss, key_dense, key_sparse, key_order = jax.random.split(key, 4)
    sparse_count = STARS_LOCAL // 8
    dense_count = STARS_LOCAL - sparse_count
    random_toss = jax.random.randint(key_toss, (TOTAL_MEASURES,), 0, 8 * MEASURES_LOCAL, dtype=jnp.int32)
    dense = jax.random.randint(key_dense, (TOTAL_MEASURES,), 0, dense_count, dtype=jnp.int32)
    sparse = jax.random.randint(key_sparse, (TOTAL_MEASURES,), dense_count, STARS_LOCAL, dtype=jnp.int32)
    raw_star = jnp.where(random_toss < STARS_LOCAL, sparse, dense)
    relabel = jax.random.permutation(key_order, STARS_LOCAL).astype(jnp.int32)
    return relabel[raw_star].astype(jnp.int32)


def place_ends(entries, stream_key, low, high):
    longest = entries.shape.index(max(entries.shape))
    spots = []
    for shift in (0, 1):
        where = [jax.random.randint(jax.random.fold_in(stream_key, axis), (), 0, length) for axis, length in enumerate(entries.shape)]
        where[longest] = (where[longest] + shift) % entries.shape[longest]
        spots.append(tuple(where))
    return entries.at[spots[0]].set(low).at[spots[1]].set(high)


def level_of(key, shape, cuts, smallest, largest):
    def one(position, parts):
        steps = jax.random.uniform(jax.random.fold_in(jax.random.fold_in(key, 6), position), (parts,), jnp.float32, smallest / len(cuts), largest / len(cuts))
        return jnp.repeat(jnp.exp(steps), shape[position] // parts).reshape((-1,) + (1,) * (len(shape) - position - 1))

    loudness = one(*cuts[0])
    for cut in cuts[1:]:
        loudness = loudness * one(*cut)
    return loudness


def deal_out(rng, own, number, rows, number_of, top, reach, lean):
    ranking = jax.random.permutation(rng, number_of)
    crowded, ordinary = load_shares(number_of, rows * top, reach, lean, True), load_shares(number_of, rows * top, reach, lean, False)
    places = jnp.arange(number_of)

    def named(lengths, rotation):
        used = int((lengths > 0).sum())
        fixed = max(1, used // 4)
        passed = fixed + (places - fixed + rotation * (used - fixed)) % max(1, number_of - fixed)
        return jnp.zeros((number_of,), jnp.int32).at[ranking[jnp.where(places < fixed, places, passed)]].set(jnp.asarray(lengths, jnp.int32))

    lengths = jnp.where(number % 4 == 0, named(crowded, number // 4), named(ordinary, number - number // 4 - 1))
    mixed = jax.random.permutation(jax.random.fold_in(own, 3), number_of)
    source_of, sink = mixed[0:number_of // 2 * 2:2], mixed[1:number_of // 2 * 2:2]
    margin = jnp.minimum(lengths[source_of] - 1, reach - lengths[sink]) // 2
    margin = jnp.where((source_of == ranking[0]) | (sink == ranking[0]) | (lengths[sink] == 0), 0, jnp.maximum(margin, 0))
    passed = jax.random.randint(jax.random.fold_in(own, 4), (number_of // 2,), 0, 1 << 20) % (margin + 1)
    lengths = lengths.at[source_of].add(-passed).at[sink].add(passed)
    labels = jnp.searchsorted(jnp.cumsum(lengths), jnp.arange(rows * top), side="right").astype(jnp.int32)
    table = labels.reshape(top, rows).T
    table = table[jax.random.permutation(jax.random.fold_in(own, 1), rows)]
    rotation = jax.random.randint(jax.random.fold_in(own, 2), (rows, 1), 0, top)
    return jnp.take_along_axis(table, (jnp.arange(top)[None, :] + rotation) % top, axis=1)


def load_shares(amount, total, bound, lean, full):
    portions = [(1 << 20) // math.isqrt(standing ** lean) + 1 for standing in range(1, amount + 1)]
    largest = bound if full else min(bound, max(-(-total // amount), total * portions[0] // sum(portions)))
    least = 1 if total - largest >= amount - 1 else 0
    counts, spare = [largest] + [least] * (amount - 1), total - largest - least * (amount - 1)
    while spare > 0:
        movable = [i for i in range(1, amount) if counts[i] < largest] or [i for i in range(1, amount) if counts[i] < bound]
        pool, remaining = sum([portions[i] for i in movable]), spare
        for i in movable:
            more = min(bound - counts[i], max(1, remaining * portions[i] // pool), spare)
            counts[i] = counts[i] + more
            spare = spare - more
    return np.array(counts)


def noise(own_key, extent, spread, most, cuts=(), kind=jnp.bfloat16):
    loudness = level_of(own_key, extent, cuts, -0.22, 0.18) if cuts else 1.0
    values = jax.random.normal(own_key, extent, jnp.float32) * spread * loudness
    return jnp.minimum(jnp.maximum(values, -most), most).astype(kind)


def setup_inputs(seed: int = 0) -> dict:
    arg_keys = jax.random.split(jax.random.key(seed), 8)
    measure_plane = jnp.clip(jax.random.uniform(arg_keys[0], (2, TOTAL_MEASURES), jnp.float32, -1.0, 1.0) * level_of(arg_keys[0], (2, TOTAL_MEASURES), ((1, 32),), -0.4, 0.0), -1.0, 1.0)
    measure_weight = jnp.clip(jnp.exp(math.log(2.0) - 2.9957323 * jax.random.uniform(arg_keys[1], (TOTAL_MEASURES,), jnp.float32) ** level_of(arg_keys[1], (TOTAL_MEASURES,), ((0, 32),), -0.2, 0.2)), 0.1, 2.0)
    measure_visit = place_ends(jax.random.randint(arg_keys[2], (TOTAL_MEASURES,), 0, VISITS_LOCAL), jax.random.fold_in(arg_keys[2], 1), 0, VISITS_LOCAL - 1).astype(jnp.int32)
    measure_holder_keys = jax.random.split(jax.random.fold_in(arg_keys[3], 1), TOTAL_MEASURES // MEASURES_LOCAL)
    measure_holder_turns = jax.random.permutation(jax.random.fold_in(arg_keys[3], 3), TOTAL_MEASURES // MEASURES_LOCAL)
    measure_holder = jax.vmap(lambda own, number: deal_out(jax.random.fold_in(arg_keys[3], 2), own, number, MEASURES_LOCAL, N_DEV, 1, MEASURE_LIMIT, 1))(measure_holder_keys, measure_holder_turns).reshape((TOTAL_MEASURES, 1))
    measure_star = draw_measure_star(jax.random.fold_in(arg_keys[7], 71), 0)
    visit_coefficients = noise(arg_keys[5], (VISITS, 2 * NMON), 0.3, 4.0, ((0, 8),), jnp.float32)
    star_location = noise(arg_keys[6], (2, TOTAL_STARS), 1.0, 6.0, ((1, 32),), jnp.float32)
    return {"measure_plane": measure_plane, "measure_weight": measure_weight, "measure_visit": measure_visit, "measure_holder": measure_holder, "measure_star": measure_star, "visit_coefficients": visit_coefficients, "star_location": star_location}


def chebyshev(coord):
    series = [jnp.ones_like(coord), coord]
    for degree in range(2, 7):
        series.append(2.0 * coord * series[-1] - series[-2])
    return series


def jacobian_rows(u_coord, v_coord):
    cheb_u = chebyshev(u_coord)
    cheb_v = chebyshev(v_coord)
    columns = [cheb_u[order_u] * cheb_v[order_v] for order_u in range(7) for order_v in range(7 - order_u)]
    return jnp.stack(columns, axis=0)


def reference(measure_plane, measure_weight, measure_visit, measure_holder, measure_star, visit_coefficients, star_location):
    measure_tally = measure_weight.shape[0]
    holder_lookup = jnp.arange(measure_tally, dtype=jnp.int32) // MEASURES_LOCAL
    region_lookup = holder_lookup // N_DEV
    inside_region = holder_lookup % N_DEV
    visit_number = (inside_region * VISITS_LOCAL + measure_visit).astype(jnp.int32)
    star_number = ((region_lookup * N_DEV + measure_holder[:, 0]) * STARS_LOCAL + measure_star).astype(jnp.int32)
    jacobian_matrix = jacobian_rows(measure_plane[0], measure_plane[1])
    coef_rows = visit_coefficients[visit_number]
    predicted_plane = jnp.stack([jnp.sum(coef_rows[:, :NMON].T * jacobian_matrix, axis=0),
                           jnp.sum(coef_rows[:, NMON:].T * jacobian_matrix, axis=0)])
    misfit_value = predicted_plane - star_location[:, star_number]
    weight_total = jax.ops.segment_sum(measure_weight, star_number, TOTAL_STARS)
    weight_minimum = jnp.maximum(weight_total, 1.0)
    residual_total = jax.ops.segment_sum((measure_weight * misfit_value).T, star_number, TOTAL_STARS).T
    star_mean = residual_total / weight_minimum
    share_ratio = measure_weight / weight_minimum[star_number]
    offset_error = misfit_value - star_mean[:, star_number]
    normal_weight = measure_weight * (1.0 - share_ratio)
    weighted = normal_weight * jacobian_matrix
    block_rows = min(8192, measure_tally)
    block_count = measure_tally // block_rows
    weighted_blocks = weighted.reshape(NMON, block_count, block_rows).transpose(1, 0, 2)
    design_blocks = jacobian_matrix.reshape(NMON, block_count, block_rows).transpose(1, 0, 2)
    visit_blocks = visit_number.reshape(block_count, block_rows)

    def add_block(gram_total, pieces):
        weighted_block, design_block, visit_block = pieces
        outer_prod = (weighted_block[:, None, :] * design_block[None, :, :]).reshape(NMON * NMON, block_rows)
        return gram_total + jax.ops.segment_sum(outer_prod.T, visit_block, VISITS), None

    gram_start = jnp.zeros((VISITS, NMON * NMON), jnp.float32)
    gram_total, unused = lax.scan(add_block, gram_start, (weighted_blocks, design_blocks, visit_blocks))
    weighted_error = measure_weight * offset_error
    rhs_terms = (weighted_error[:, None, :] * jacobian_matrix[None, :, :]).reshape(2 * NMON, measure_tally)
    rhs_total = jax.ops.segment_sum(rhs_terms.T, visit_number, VISITS)
    rescale_unit = VISITS_LOCAL / (MEASURES_LOCAL * N_PATCH)
    return gram_total * rescale_unit, rhs_total * (rescale_unit ** 0.5), star_mean
```

```python
import functools
import math

import jax
import jax.numpy as jnp
import ml_dtypes
import numpy as np
from jax import lax
from jax.experimental import pallas as pl
from jax.experimental.pallas import tpu as pltpu
from jax.sharding import PartitionSpec as P

NMON = 28
DEG = 6
PAIRS = [(a, b) for a in range(DEG + 1) for b in range(DEG + 1 - a)]
MOMENTS = 144
ROWS = 256
COLS = 1024
RHS_COL = 896
F32 = jnp.float32
BF16 = jnp.bfloat16
MESH = pl.DeviceIdType.MESH
NT = (((1,), (1,)), ((), ()))
NN = (((1,), (0,)), ((), ()))


def moment_row(p, q):
    return 16 * p + q if p <= 4 else 80 + 8 * (p - 5) + q


def expansion():
    table = np.zeros((ROWS, COLS), np.float32)
    for k, (a, b) in enumerate(PAIRS):
        for l, (c, d) in enumerate(PAIRS):
            for p in (a + c, abs(a - c)):
                for q in (b + d, abs(b - d)):
                    table[moment_row(p, q), k * NMON + l] += 0.25
        for c in range(2):
            table[MOMENTS + c * 56 + a * 8 + b, RHS_COL + c * NMON + k] = 1.0
    return table.astype(ml_dtypes.bfloat16)


def coefficient_spread():
    table = np.zeros((112, 2 * NMON), np.float32)
    for k, (a, b) in enumerate(PAIRS):
        for c in range(2):
            table[c * 56 + a * 8 + b, c * NMON + k] = 1.0
    return table.astype(ml_dtypes.bfloat16)


def split3(x):
    high = x.astype(BF16)
    rest = x - high.astype(F32)
    middle = rest.astype(BF16)
    return high, middle, (rest - middle.astype(F32)).astype(BF16)


def dot(a, b, dims):
    return lax.dot_general(a, b, dims, preferred_element_type=F32)


def three(total, rows):
    return total[:rows] + total[rows : 2 * rows] + total[2 * rows : 3 * rows]


def kernel(
    n_dev,
    n_patch,
    scale,
    plane_ref,
    weight_ref,
    visit_ref,
    holder_ref,
    star_ref,
    coef_ref,
    loc_ref,
    spread_ref,
    expand_hbm,
    blocks_ref,
    rhs_ref,
    offset_ref,
    expand_ref,
    tu_ref,
    tv_ref,
    loc_tile,
    part_ref,
    part_in,
    table_ref,
    moment_ref,
    moment_in,
    sum_ref,
    expand_sem,
    send_a,
    recv_a,
    send_b,
    recv_b,
    send_c,
    recv_c,
    send_d,
    recv_d,
):
    me_d = lax.axis_index("dev")
    me_p = lax.axis_index("patch")
    barrier = pltpu.get_barrier_semaphore()
    for j in range(1, n_dev):
        pl.semaphore_signal(
            barrier, inc=1, device_id={"dev": lax.rem(me_d + j, n_dev)}, device_id_type=MESH
        )
    for j in range(1, n_patch):
        pl.semaphore_signal(
            barrier, inc=1, device_id={"patch": lax.rem(me_p + j, n_patch)}, device_id_type=MESH
        )
    expand_copy = pltpu.make_async_copy(expand_hbm, expand_ref, expand_sem)
    expand_copy.start()

    rows = weight_ref.shape[1]
    visits = coef_ref.shape[0]
    weight = weight_ref[...]
    coords = plane_ref[...]
    series = [jnp.ones_like(coords), coords]
    for degree in range(2, 13):
        series.append(2.0 * coords * series[-1] - series[-2])
    tv_ref[...] = jnp.zeros_like(tv_ref)
    for degree, value in enumerate(series):
        tu_ref[degree : degree + 1, :] = value[0:1]
        tv_ref[degree : degree + 1, :] = value[1:2]

    def basis(a, group):
        return tu_ref[a : a + 1, :] * tv_ref[8 * group : 8 * group + 8, :]

    visit_hot = jnp.where(
        lax.broadcasted_iota(jnp.int32, (visits, rows), 0) == visit_ref[...], 1.0, 0.0
    ).astype(BF16)
    coef = jnp.concatenate(
        [dot(spread_ref[...], piece, NT) for piece in split3(coef_ref[...])], axis=0
    ).astype(BF16)
    picked = three(dot(coef, visit_hot, NN), 112)
    predicted = []
    for c in range(2):
        total = picked[c * 56 : c * 56 + 8] * basis(0, 0)
        for a in range(1, 7):
            total = total + picked[c * 56 + 8 * a : c * 56 + 8 * a + 8] * basis(a, 0)
        predicted.append(jnp.sum(total, axis=0, keepdims=True))

    star = star_ref[...]
    low = lax.rem(star, 128)
    place = holder_ref[...] * 2 + lax.div(star, 128)
    low_hot = jnp.where(
        lax.broadcasted_iota(jnp.int32, (128, rows), 0) == low, 1.0, 0.0
    ).astype(BF16)
    sub = lax.broadcasted_iota(jnp.int32, (8, rows), 0)
    half = lax.div(sub, 4)
    kind = lax.rem(sub, 4)
    values = jnp.where(
        kind == 0,
        weight,
        jnp.where(
            kind == 1,
            weight * predicted[0],
            jnp.where(kind == 2, weight * predicted[1], 0.0),
        ),
    )
    here = place - half
    masked = []
    for piece in split3(values):
        piece = piece.astype(F32)
        masked += [jnp.where(here == 2 * d, piece, 0.0) for d in range(n_dev)]
    sums = three(
        dot(jnp.concatenate(masked, axis=0).astype(BF16), low_hot, NT), 8 * n_dev
    )
    for d in range(n_dev):
        part_ref[d] = sums[8 * d : 8 * d + 8]
    loc_tile[...] = jnp.zeros_like(loc_tile)
    for h in range(2):
        for c in range(2):
            loc_tile[4 * h + 1 + c : 4 * h + 2 + c, :] = loc_ref[
                c : c + 1, 128 * h : 128 * h + 128
            ]

    pl.semaphore_wait(barrier, n_dev + n_patch - 2)
    scatter = []
    for j in range(1, n_dev):
        peer = lax.rem(me_d + j, n_dev)
        copy = pltpu.make_async_remote_copy(
            src_ref=part_ref.at[peer],
            dst_ref=part_in.at[j - 1],
            send_sem=send_a.at[j - 1],
            recv_sem=recv_a.at[j - 1],
            device_id={"dev": peer},
            device_id_type=MESH,
        )
        copy.start()
        scatter.append(copy)
    star_total = part_ref[me_d]
    for j in range(1, n_dev):
        scatter[j - 1].wait_recv()
        star_total = star_total + part_in[j - 1]

    tile_row = lax.broadcasted_iota(jnp.int32, (8, 128), 0)
    mass = jnp.where(tile_row < 4, star_total[0:1], star_total[4:5])
    floor = jnp.maximum(mass, 1.0)
    location = loc_tile[...]
    offset = (star_total - mass * location) / floor
    table_ref[me_d] = jnp.where(
        lax.rem(tile_row, 4) == 0, 1.0 / floor, location + offset
    )
    gather = []
    for j in range(1, n_dev):
        copy = pltpu.make_async_remote_copy(
            src_ref=table_ref.at[me_d],
            dst_ref=table_ref.at[me_d],
            send_sem=send_b.at[j - 1],
            recv_sem=recv_b.at[j - 1],
            device_id={"dev": lax.rem(me_d + j, n_dev)},
            device_id_type=MESH,
        )
        copy.start()
        gather.append(copy)
    for h in range(2):
        for c in range(2):
            offset_ref[c : c + 1, 128 * h : 128 * h + 128] = offset[
                4 * h + 1 + c : 4 * h + 2 + c
            ]
    for copy in gather:
        copy.wait_recv()
    table = table_ref[...].reshape(8 * n_dev, 128)
    found = three(
        dot(jnp.concatenate(split3(table), axis=0), low_hot, NN), 8 * n_dev
    )
    chosen = jnp.where(here == 0, found[0:8], 0.0)
    for d in range(1, n_dev):
        chosen = chosen + jnp.where(here == 2 * d, found[8 * d : 8 * d + 8], 0.0)
    chosen = chosen[0:4] + chosen[4:8]
    normal = weight * (1.0 - weight * chosen[0:1])
    error = [weight * (predicted[c] - chosen[1 + c : 2 + c]) for c in range(2)]

    stack = []
    for a in range(13):
        stack += [normal * basis(a, group) for group in range(2 if a <= 4 else 1)]
    for c in range(2):
        stack += [error[c] * basis(a, 0) for a in range(7)]
    pieces = jnp.concatenate(split3(jnp.concatenate(stack, axis=0)), axis=0)
    moments = three(dot(pieces, visit_hot, NT), ROWS)
    packed = jnp.concatenate([moments[:128], moments[128:]], axis=1)
    share = 128 // n_patch
    for q in range(n_patch):
        moment_ref[q] = packed[q * share : (q + 1) * share]
    scatter_p = []
    for j in range(1, n_patch):
        peer = lax.rem(me_p + j, n_patch)
        copy = pltpu.make_async_remote_copy(
            src_ref=moment_ref.at[peer],
            dst_ref=moment_in.at[j - 1],
            send_sem=send_c.at[j - 1],
            recv_sem=recv_c.at[j - 1],
            device_id={"patch": peer},
            device_id_type=MESH,
        )
        copy.start()
        scatter_p.append(copy)
    total = moment_ref[me_p]
    for j in range(1, n_patch):
        scatter_p[j - 1].wait_recv()
        total = total + moment_in[j - 1]
    sum_ref[me_p] = total
    gather_p = []
    for j in range(1, n_patch):
        copy = pltpu.make_async_remote_copy(
            src_ref=sum_ref.at[me_p],
            dst_ref=sum_ref.at[me_p],
            send_sem=send_d.at[j - 1],
            recv_sem=recv_d.at[j - 1],
            device_id={"patch": lax.rem(me_p + j, n_patch)},
            device_id_type=MESH,
        )
        copy.start()
        gather_p.append(copy)
    expand_copy.wait()
    for copy in gather_p:
        copy.wait_recv()
    turned = sum_ref[...].reshape(128, 128).T
    left = jnp.concatenate(split3(turned[:visits]), axis=0)
    right = jnp.concatenate(split3(turned[visits:]), axis=0)
    result = three(
        dot(left, expand_ref[:128, :], NN) + dot(right, expand_ref[128:, :], NN), visits
    )
    blocks_ref[...] = result[:, : NMON * NMON] * scale
    rhs_ref[...] = result[:, RHS_COL : RHS_COL + 2 * NMON] * math.sqrt(scale)
    for copy in scatter + gather + scatter_p + gather_p:
        copy.wait_send()


def per_device(n_dev, n_patch, plane, weight, visit, holder, star, coef, loc):
    rows = weight.shape[0]
    visits = coef.shape[0]
    scale = visits / (rows * n_patch)
    share = 128 // n_patch
    vmem = pl.BlockSpec(memory_space=pltpu.VMEM)
    dma = pltpu.SemaphoreType.DMA
    return tuple(
        pl.pallas_call(
            functools.partial(kernel, n_dev, n_patch, scale),
            out_shape=(
                jax.ShapeDtypeStruct((visits, NMON * NMON), F32),
                jax.ShapeDtypeStruct((visits, 2 * NMON), F32),
                jax.ShapeDtypeStruct(loc.shape, F32),
            ),
            in_specs=[vmem] * 8 + [pl.BlockSpec(memory_space=pl.ANY)],
            out_specs=(vmem, vmem, vmem),
            scratch_shapes=[
                pltpu.VMEM((ROWS, COLS), BF16),
                pltpu.VMEM((16, rows), F32),
                pltpu.VMEM((16, rows), F32),
                pltpu.VMEM((8, 128), F32),
                pltpu.VMEM((n_dev, 8, 128), F32),
                pltpu.VMEM((n_dev - 1, 8, 128), F32),
                pltpu.VMEM((n_dev, 8, 128), F32),
                pltpu.VMEM((n_patch, share, 128), F32),
                pltpu.VMEM((n_patch - 1, share, 128), F32),
                pltpu.VMEM((n_patch, share, 128), F32),
                dma,
                dma((n_dev - 1,)),
                dma((n_dev - 1,)),
                dma((n_dev - 1,)),
                dma((n_dev - 1,)),
                dma((n_patch - 1,)),
                dma((n_patch - 1,)),
                dma((n_patch - 1,)),
                dma((n_patch - 1,)),
            ],
            compiler_params=pltpu.CompilerParams(
                collective_id=0, has_side_effects=True, vmem_limit_bytes=40 * 1024 * 1024
            ),
        )(
            plane,
            weight.reshape(1, rows),
            visit.reshape(1, rows),
            holder.reshape(1, rows),
            star.reshape(1, rows),
            coef,
            loc,
            jnp.asarray(coefficient_spread()),
            jnp.asarray(expansion()),
        )
    )


def solution(mesh):
    placed = (
        P(None, ("patch", "dev")),
        P(("patch", "dev")),
        P(("patch", "dev")),
        P(("patch", "dev"), None),
        P(("patch", "dev")),
        P("dev", None),
        P(None, ("patch", "dev")),
    )
    return jax.shard_map(
        functools.partial(per_device, mesh.shape["dev"], mesh.shape["patch"]),
        mesh=mesh,
        in_specs=placed,
        out_specs=(P("dev", None), P("dev", None), P(None, ("patch", "dev"))),
        check_vma=False,
    )
```

```python
import functools
import math

import jax
import jax.numpy as jnp
import ml_dtypes
import numpy as np
from jax import lax
from jax.experimental import pallas as pl
from jax.experimental.pallas import tpu as pltpu
from jax.sharding import PartitionSpec as P

NMON = 28
DEG = 6
PAIRS = [(a, b) for a in range(DEG + 1) for b in range(DEG + 1 - a)]
MOMENTS = 144
ROWS = 256
COLS = 1024
RHS_COL = 896
F32 = jnp.float32
BF16 = jnp.bfloat16
MESH = pl.DeviceIdType.MESH
CHUNK = 2048
TWO = True
NT = (((1,), (1,)), ((), ()))
NN = (((1,), (0,)), ((), ()))


def moment_row(p, q):
    return 16 * p + q if p <= 4 else 80 + 8 * (p - 5) + q


def expansion():
    table = np.zeros((ROWS, COLS), np.float32)
    for k, (a, b) in enumerate(PAIRS):
        for l, (c, d) in enumerate(PAIRS):
            for p in (a + c, abs(a - c)):
                for q in (b + d, abs(b - d)):
                    table[moment_row(p, q), k * NMON + l] += 0.25
        for c in range(2):
            table[MOMENTS + c * 56 + a * 8 + b, RHS_COL + c * NMON + k] = 1.0
    return table.astype(ml_dtypes.bfloat16)


def coefficient_spread():
    table = np.zeros((112, 2 * NMON), np.float32)
    for k, (a, b) in enumerate(PAIRS):
        for c in range(2):
            table[c * 56 + a * 8 + b, c * NMON + k] = 1.0
    return table.astype(ml_dtypes.bfloat16)


def split3(x):
    high = x.astype(BF16)
    rest = x - high.astype(F32)
    middle = rest.astype(BF16)
    return high, middle, (rest - middle.astype(F32)).astype(BF16)


def dot(a, b, dims):
    return lax.dot_general(a, b, dims, preferred_element_type=F32)


def three(total, rows):
    return total[:rows] + total[rows : 2 * rows] + total[2 * rows : 3 * rows]


def widen(scale, visits, packed, expand_ref, blocks_ref, rhs_ref):
    turned = packed.T
    left = jnp.concatenate(split3(turned[:visits]), axis=0)
    right = jnp.concatenate(split3(turned[visits:]), axis=0)
    result = three(
        dot(left, expand_ref[:128, :], NN) + dot(right, expand_ref[128:, :], NN), visits
    )
    blocks_ref[...] = result[:, : NMON * NMON] * scale
    ends = jnp.concatenate([result[:, RHS_COL:]] * 2, axis=0).T
    rhs_ref[...] = ends[: 2 * NMON, :visits] * math.sqrt(scale)


def expand_kernel(
    scale,
    visits,
    total_hbm,
    offset_hbm,
    expand_hbm,
    blocks_ref,
    rhs_ref,
    offset_out,
    total_ref,
    expand_ref,
    sems,
):
    copies = [
        pltpu.make_async_copy(source, target, sems.at[i])
        for i, (source, target) in enumerate(
            ((total_hbm, total_ref), (expand_hbm, expand_ref), (offset_hbm, offset_out))
        )
    ]
    for copy in copies:
        copy.start()
    for copy in copies[:2]:
        copy.wait()
    widen(scale, visits, total_ref[...], expand_ref, blocks_ref, rhs_ref)
    copies[2].wait()


def kernel(n_dev, n_patch, scale, *refs):
    sources, refs = refs[:9], refs[9:]
    if TWO:
        (total_ref, offset_ref), refs = refs[:2], refs[2:]
    else:
        (blocks_ref, rhs_ref, offset_ref), refs = refs[:3], refs[3:]
    held, refs = refs[:9], refs[9:]
    plane_ref, weight_ref, visit_ref, holder_ref, star_ref, coef_ref, loc_ref, spread_ref, expand_ref = held
    tu_ref, tv_ref, loc_tile, part_ref, part_in, table_ref, moment_ref, moment_in, sum_ref, load_sem = refs[:10]
    send_a, recv_a, send_b, recv_b, send_c, recv_c, send_d, recv_d = refs[10:]
    loads = [
        pltpu.make_async_copy(source, target, load_sem.at[i])
        for i, (source, target) in enumerate(zip(sources, held))
        if i < 8 or not TWO
    ]
    for load in loads:
        load.start()
    me_d = lax.axis_index("dev")
    me_p = lax.axis_index("patch")
    barrier = pltpu.get_barrier_semaphore()
    for j in range(1, n_dev):
        pl.semaphore_signal(
            barrier, inc=1, device_id={"dev": lax.rem(me_d + j, n_dev)}, device_id_type=MESH
        )
    for j in range(1, n_patch):
        pl.semaphore_signal(
            barrier, inc=1, device_id={"patch": lax.rem(me_p + j, n_patch)}, device_id_type=MESH
        )
    for load in loads[:8]:
        load.wait()

    rows = weight_ref.shape[1]
    visits = coef_ref.shape[1]
    weight = weight_ref[...]
    coords = plane_ref[...]
    series = [jnp.ones_like(coords), coords]
    for degree in range(2, 13):
        series.append(2.0 * coords * series[-1] - series[-2])
    tv_ref[...] = jnp.zeros_like(tv_ref)
    for degree, value in enumerate(series):
        tu_ref[degree : degree + 1, :] = value[0:1]
        tv_ref[degree : degree + 1, :] = value[1:2]

    coef = jnp.concatenate(
        [dot(spread_ref[...], piece, NN) for piece in split3(coef_ref[...])], axis=0
    ).astype(BF16)
    width = min(CHUNK, rows)
    sub = lax.broadcasted_iota(jnp.int32, (8, width), 0)
    half = lax.div(sub, 4)
    kind = lax.rem(sub, 4)
    sums = jnp.zeros((8 * n_dev, 128), F32)
    kept = []
    for start in range(0, rows, width):
        at = slice(start, start + width)

        def basis(a, group, at=at):
            return tu_ref[a : a + 1, at] * tv_ref[8 * group : 8 * group + 8, at]

        visit_hot = jnp.where(
            lax.broadcasted_iota(jnp.int32, (visits, width), 0) == visit_ref[:, at], 1.0, 0.0
        ).astype(BF16)
        picked = three(dot(coef, visit_hot, NN), 112)
        predicted = []
        for c in range(2):
            total = picked[c * 56 : c * 56 + 8] * basis(0, 0)
            for a in range(1, 7):
                total = total + picked[c * 56 + 8 * a : c * 56 + 8 * a + 8] * basis(a, 0)
            predicted.append(jnp.sum(total, axis=0, keepdims=True))
        star = star_ref[:, at]
        weight = weight_ref[:, at]
        place = holder_ref[:, at] * 2 + lax.div(star, 128)
        low_hot = jnp.where(
            lax.broadcasted_iota(jnp.int32, (128, width), 0) == lax.rem(star, 128), 1.0, 0.0
        ).astype(BF16)
        values = jnp.where(
            kind == 0,
            weight,
            jnp.where(
                kind == 1,
                weight * predicted[0],
                jnp.where(kind == 2, weight * predicted[1], 0.0),
            ),
        )
        here = place - half
        masked = []
        for piece in split3(values):
            piece = piece.astype(F32)
            masked += [jnp.where(here == 2 * d, piece, 0.0) for d in range(n_dev)]
        sums = sums + three(
            dot(jnp.concatenate(masked, axis=0).astype(BF16), low_hot, NT), 8 * n_dev
        )
        kept.append((basis, visit_hot, low_hot, predicted, weight, here))
    for d in range(n_dev):
        part_ref[d] = sums[8 * d : 8 * d + 8]
    loc_tile[...] = jnp.zeros_like(loc_tile)
    for h in range(2):
        for c in range(2):
            loc_tile[4 * h + 1 + c : 4 * h + 2 + c, :] = loc_ref[
                c : c + 1, 128 * h : 128 * h + 128
            ]

    pl.semaphore_wait(barrier, n_dev + n_patch - 2)
    scatter = []
    for j in range(1, n_dev):
        peer = lax.rem(me_d + j, n_dev)
        copy = pltpu.make_async_remote_copy(
            src_ref=part_ref.at[peer],
            dst_ref=part_in.at[j - 1],
            send_sem=send_a.at[j - 1],
            recv_sem=recv_a.at[j - 1],
            device_id={"dev": peer},
            device_id_type=MESH,
        )
        copy.start()
        scatter.append(copy)
    star_total = part_ref[me_d]
    for j in range(1, n_dev):
        scatter[j - 1].wait_recv()
        star_total = star_total + part_in[j - 1]

    tile_row = lax.broadcasted_iota(jnp.int32, (8, 128), 0)
    mass = jnp.where(tile_row < 4, star_total[0:1], star_total[4:5])
    floor = jnp.maximum(mass, 1.0)
    location = loc_tile[...]
    offset = (star_total - mass * location) / floor
    table_ref[me_d] = jnp.where(
        lax.rem(tile_row, 4) == 0, 1.0 / floor, location + offset
    )
    gather = []
    for j in range(1, n_dev):
        copy = pltpu.make_async_remote_copy(
            src_ref=table_ref.at[me_d],
            dst_ref=table_ref.at[me_d],
            send_sem=send_b.at[j - 1],
            recv_sem=recv_b.at[j - 1],
            device_id={"dev": lax.rem(me_d + j, n_dev)},
            device_id_type=MESH,
        )
        copy.start()
        gather.append(copy)
    for h in range(2):
        for c in range(2):
            offset_ref[c : c + 1, 128 * h : 128 * h + 128] = offset[
                4 * h + 1 + c : 4 * h + 2 + c
            ]
    for copy in gather:
        copy.wait_recv()
    table = table_ref[...].reshape(8 * n_dev, 128)
    table = jnp.concatenate(split3(table), axis=0)
    wide = jnp.zeros((MOMENTS, visits), F32)
    side = jnp.zeros((ROWS - MOMENTS, visits), F32)
    for basis, visit_hot, low_hot, predicted, weight, here in kept:
        found = three(dot(table, low_hot, NN), 8 * n_dev)
        chosen = jnp.where(here == 0, found[0:8], 0.0)
        for d in range(1, n_dev):
            chosen = chosen + jnp.where(here == 2 * d, found[8 * d : 8 * d + 8], 0.0)
        chosen = chosen[0:4] + chosen[4:8]
        normal = weight * (1.0 - weight * chosen[0:1])
        error = [weight * (predicted[c] - chosen[1 + c : 2 + c]) for c in range(2)]
        stack = []
        for a in range(13):
            stack += [normal * basis(a, group) for group in range(2 if a <= 4 else 1)]
        pieces = split3(jnp.concatenate(stack, axis=0))[:2]
        stack = []
        for c in range(2):
            stack += [error[c] * basis(a, 0) for a in range(7)]
        pieces += split3(jnp.concatenate(stack, axis=0))
        both = dot(jnp.concatenate(pieces, axis=0), visit_hot, NT)
        wide = wide + both[:MOMENTS] + both[MOMENTS : 2 * MOMENTS]
        side = side + three(both[2 * MOMENTS :], ROWS - MOMENTS)
    moments = jnp.concatenate([wide, side], axis=0)
    packed = jnp.concatenate([moments[:128], moments[128:]], axis=1)
    share = 128 // n_patch
    for q in range(n_patch):
        moment_ref[q] = packed[q * share : (q + 1) * share]
    scatter_p = []
    for j in range(1, n_patch):
        peer = lax.rem(me_p + j, n_patch)
        copy = pltpu.make_async_remote_copy(
            src_ref=moment_ref.at[peer],
            dst_ref=moment_in.at[j - 1],
            send_sem=send_c.at[j - 1],
            recv_sem=recv_c.at[j - 1],
            device_id={"patch": peer},
            device_id_type=MESH,
        )
        copy.start()
        scatter_p.append(copy)
    total = moment_ref[me_p]
    for j in range(1, n_patch):
        scatter_p[j - 1].wait_recv()
        total = total + moment_in[j - 1]
    sum_ref[me_p] = total
    gather_p = []
    for j in range(1, n_patch):
        copy = pltpu.make_async_remote_copy(
            src_ref=sum_ref.at[me_p],
            dst_ref=sum_ref.at[me_p],
            send_sem=send_d.at[j - 1],
            recv_sem=recv_d.at[j - 1],
            device_id={"patch": lax.rem(me_p + j, n_patch)},
            device_id_type=MESH,
        )
        copy.start()
        gather_p.append(copy)
    if not TWO:
        loads[8].wait()
    for copy in gather_p:
        copy.wait_recv()
    if TWO:
        total_ref[...] = sum_ref[...].reshape(128, 128)
    else:
        widen(scale, visits, sum_ref[...].reshape(128, 128), expand_ref, blocks_ref, rhs_ref)
    for copy in scatter + gather + scatter_p + gather_p:
        copy.wait_send()


def per_device(n_dev, n_patch, plane, weight, visit, holder, star, coef, loc):
    rows = weight.shape[0]
    visits = coef.shape[0]
    scale = visits / (rows * n_patch)
    share = 128 // n_patch
    vmem = pl.BlockSpec(memory_space=pltpu.VMEM)
    dma = pltpu.SemaphoreType.DMA
    args = (
        plane,
        weight.reshape(1, rows),
        visit.reshape(1, rows),
        holder.reshape(1, rows),
        star.reshape(1, rows),
        coef.T,
        loc,
        jnp.asarray(coefficient_spread()),
        jnp.asarray(expansion()),
    )
    final = (
        jax.ShapeDtypeStruct((visits, NMON * NMON), F32),
        jax.ShapeDtypeStruct((2 * NMON, visits), F32),
        jax.ShapeDtypeStruct(loc.shape, F32),
    )
    first = (jax.ShapeDtypeStruct((128, 128), F32), final[2]) if TWO else final
    outs = pl.pallas_call(
        functools.partial(kernel, n_dev, n_patch, scale),
        out_shape=first,
        in_specs=[pl.BlockSpec(memory_space=pltpu.HBM)] * 9,
        out_specs=(vmem,) * len(first),
        scratch_shapes=[pltpu.VMEM(x.shape, x.dtype) for x in args]
        + [
            pltpu.VMEM((16, rows), F32),
            pltpu.VMEM((16, rows), F32),
            pltpu.VMEM((8, 128), F32),
            pltpu.VMEM((n_dev, 8, 128), F32),
            pltpu.VMEM((n_dev - 1, 8, 128), F32),
            pltpu.VMEM((n_dev, 8, 128), F32),
            pltpu.VMEM((n_patch, share, 128), F32),
            pltpu.VMEM((n_patch - 1, share, 128), F32),
            pltpu.VMEM((n_patch, share, 128), F32),
            dma((9,)),
        ]
        + [dma((n_dev - 1,))] * 4
        + [dma((n_patch - 1,))] * 4,
        compiler_params=pltpu.CompilerParams(
            collective_id=0, has_side_effects=True, vmem_limit_bytes=62 * 1024 * 1024
        ),
    )(*args)
    if TWO:
        outs = pl.pallas_call(
            functools.partial(expand_kernel, scale, visits),
            out_shape=final,
            in_specs=[pl.BlockSpec(memory_space=pltpu.HBM)] * 3,
            out_specs=(vmem, vmem, pl.BlockSpec(memory_space=pltpu.HBM)),
            scratch_shapes=[
                pltpu.VMEM((128, 128), F32),
                pltpu.VMEM((ROWS, COLS), BF16),
                dma((3,)),
            ],
            compiler_params=pltpu.CompilerParams(vmem_limit_bytes=62 * 1024 * 1024),
        )(outs[0], outs[1], args[8])
    return outs[0], outs[1].T, outs[2]


def solution(mesh):
    placed = (
        P(None, ("patch", "dev")),
        P(("patch", "dev")),
        P(("patch", "dev")),
        P(("patch", "dev"), None),
        P(("patch", "dev")),
        P("dev", None),
        P(None, ("patch", "dev")),
    )
    return jax.shard_map(
        functools.partial(per_device, mesh.shape["dev"], mesh.shape["patch"]),
        mesh=mesh,
        in_specs=placed,
        out_specs=(P("dev", None), P("dev", None), P(None, ("patch", "dev"))),
        check_vma=False,
    )
```

```python
import functools
import math

import jax
import jax.numpy as jnp
import ml_dtypes
import numpy as np
from jax import lax
from jax.experimental import pallas as pl
from jax.experimental.pallas import tpu as pltpu
from jax.sharding import PartitionSpec as P

NMON = 28
DEG = 6
PAIRS = [(a, b) for a in range(DEG + 1) for b in range(DEG + 1 - a)]
MOMENTS = 144
ROWS = 256
COLS = 1024
RHS_COL = 896
F32 = jnp.float32
BF16 = jnp.bfloat16
MESH = pl.DeviceIdType.MESH
CHUNK = 2048
NT = (((1,), (1,)), ((), ()))
NN = (((1,), (0,)), ((), ()))


def moment_row(p, q):
    return 16 * p + q if p <= 4 else 80 + 8 * (p - 5) + q


HALF = 80


def packing():
    runs, end = [], 0
    for p in range(13):
        runs.append((end, moment_row(p, 0), 13 - p))
        end += 13 - p
    for c in range(2):
        for a in range(DEG + 1):
            runs.append((end, MOMENTS + c * 56 + a * 8, DEG + 1 - a))
            end += DEG + 1 - a
    return runs, end


def expansion():
    place = np.zeros((ROWS,), np.int32)
    for to, source, count in packing()[0]:
        for i in range(count):
            row = to + i
            place[source + i] = row if row < HALF else 128 + row - HALF
    table = np.zeros((ROWS, COLS), np.float32)
    for k, (a, b) in enumerate(PAIRS):
        for l, (c, d) in enumerate(PAIRS):
            for p in (a + c, abs(a - c)):
                for q in (b + d, abs(b - d)):
                    table[place[moment_row(p, q)], k * NMON + l] += 0.25
        for c in range(2):
            table[place[MOMENTS + c * 56 + a * 8 + b], RHS_COL + c * NMON + k] = 1.0
    return table.astype(ml_dtypes.bfloat16)


def coefficient_spread():
    table = np.zeros((112, 2 * NMON), np.float32)
    for k, (a, b) in enumerate(PAIRS):
        for c in range(2):
            table[c * 56 + a * 8 + b, c * NMON + k] = 1.0
    return table.astype(ml_dtypes.bfloat16)


def split3(x):
    high = x.astype(BF16)
    rest = x - high.astype(F32)
    middle = rest.astype(BF16)
    return high, middle, (rest - middle.astype(F32)).astype(BF16)


def dot(a, b, dims):
    return lax.dot_general(a, b, dims, preferred_element_type=F32)


def three(total, rows):
    return total[:rows] + total[rows : 2 * rows] + total[2 * rows : 3 * rows]


def widen(scale, visits, packed, expand_ref, blocks_ref, rhs_ref):
    turned = jnp.concatenate([packed, jnp.zeros((128 - HALF, 128), F32)], axis=0).T
    left = jnp.concatenate(split3(turned[:visits]), axis=0)
    right = jnp.concatenate(split3(turned[visits:]), axis=0)
    result = three(
        dot(left, expand_ref[:128, :], NN) + dot(right, expand_ref[128:, :], NN), visits
    )
    blocks_ref[...] = result[:, : NMON * NMON] * scale
    ends = jnp.concatenate([result[:, RHS_COL:]] * 2, axis=0).T
    rhs_ref[...] = ends[: 2 * NMON, :visits] * math.sqrt(scale)


def expand_kernel(
    scale,
    visits,
    total_hbm,
    offset_hbm,
    expand_hbm,
    blocks_ref,
    rhs_ref,
    offset_out,
    total_ref,
    expand_ref,
    sems,
):
    copies = [
        pltpu.make_async_copy(source, target, sems.at[i])
        for i, (source, target) in enumerate(
            ((total_hbm, total_ref), (expand_hbm, expand_ref), (offset_hbm, offset_out))
        )
    ]
    for copy in copies:
        copy.start()
    for copy in copies[:2]:
        copy.wait()
    widen(scale, visits, total_ref[...], expand_ref, blocks_ref, rhs_ref)
    copies[2].wait()


def kernel(n_dev, n_patch, *refs):
    sources, refs = refs[:8], refs[8:]
    (total_ref, offset_ref), refs = refs[:2], refs[2:]
    held, refs = refs[:8], refs[8:]
    plane_ref, weight_ref, visit_ref, holder_ref, star_ref, coef_ref, loc_ref, spread_ref = held
    tu_ref, tv_ref, loc_tile, part_ref, shift_ref, line_ref, moment_ref, load_sem = refs[:8]
    send_a, recv_a, send_c, recv_c = refs[8:]
    loads = [
        pltpu.make_async_copy(source, target, load_sem.at[i])
        for i, (source, target) in enumerate(zip(sources, held))
    ]
    for load in loads:
        load.start()
    me_d = lax.axis_index("dev")
    me_p = lax.axis_index("patch")
    barrier = pltpu.get_barrier_semaphore()
    for j in range(1, n_dev):
        pl.semaphore_signal(
            barrier, inc=1, device_id={"dev": lax.rem(me_d + j, n_dev)}, device_id_type=MESH
        )
    for j in range(1, n_patch):
        pl.semaphore_signal(
            barrier, inc=1, device_id={"patch": lax.rem(me_p + j, n_patch)}, device_id_type=MESH
        )
    for load in loads:
        load.wait()

    rows = weight_ref.shape[1]
    visits = coef_ref.shape[1]
    weight = weight_ref[...]
    coords = plane_ref[...]
    series = [jnp.ones_like(coords), coords]
    for degree in range(2, 13):
        series.append(2.0 * coords * series[-1] - series[-2])
    tv_ref[...] = jnp.zeros_like(tv_ref)
    for degree, value in enumerate(series):
        tu_ref[degree : degree + 1, :] = value[0:1]
        tv_ref[degree : degree + 1, :] = value[1:2]

    coef = jnp.concatenate(
        [dot(spread_ref[...], piece, NN) for piece in split3(coef_ref[...])], axis=0
    ).astype(BF16)
    width = min(CHUNK, rows)
    sub = lax.broadcasted_iota(jnp.int32, (8, width), 0)
    half = lax.div(sub, 4)
    kind = lax.rem(sub, 4)
    sums = jnp.zeros((8 * n_dev, 128), F32)
    kept = []
    for start in range(0, rows, width):
        at = slice(start, start + width)

        def basis(a, group, at=at):
            return tu_ref[a : a + 1, at] * tv_ref[8 * group : 8 * group + 8, at]

        visit_hot = jnp.where(
            lax.broadcasted_iota(jnp.int32, (visits, width), 0) == visit_ref[:, at], 1.0, 0.0
        ).astype(BF16)
        picked = three(dot(coef, visit_hot, NN), 112)
        predicted = []
        for c in range(2):
            total = picked[c * 56 : c * 56 + 8] * basis(0, 0)
            for a in range(1, 7):
                total = total + picked[c * 56 + 8 * a : c * 56 + 8 * a + 8] * basis(a, 0)
            predicted.append(jnp.sum(total, axis=0, keepdims=True))
        star = star_ref[:, at]
        weight = weight_ref[:, at]
        place = holder_ref[:, at] * 2 + lax.div(star, 128)
        low_hot = jnp.where(
            lax.broadcasted_iota(jnp.int32, (128, width), 0) == lax.rem(star, 128), 1.0, 0.0
        ).astype(BF16)
        values = jnp.where(
            kind == 0,
            weight,
            jnp.where(
                kind == 1,
                weight * predicted[0],
                jnp.where(kind == 2, weight * predicted[1], 0.0),
            ),
        )
        here = place - half
        masked = []
        for piece in split3(values):
            piece = piece.astype(F32)
            masked += [jnp.where(here == 2 * d, piece, 0.0) for d in range(n_dev)]
        sums = sums + three(
            dot(jnp.concatenate(masked, axis=0).astype(BF16), low_hot, NT), 8 * n_dev
        )
        kept.append((basis, visit_hot, low_hot, predicted, weight, here))
    for d in range(n_dev):
        part_ref[me_d, d] = sums[8 * d : 8 * d + 8]
    loc_tile[...] = jnp.zeros_like(loc_tile)
    for h in range(2):
        for c in range(2):
            loc_tile[4 * h + 1 + c : 4 * h + 2 + c, :] = loc_ref[
                c : c + 1, 128 * h : 128 * h + 128
            ]

    pl.semaphore_wait(barrier, n_dev + n_patch - 2)
    part_ref[me_d, n_dev] = loc_tile[...]
    gather = []
    for j in range(1, n_dev):
        copy = pltpu.make_async_remote_copy(
            src_ref=part_ref.at[me_d],
            dst_ref=part_ref.at[me_d],
            send_sem=send_a.at[j - 1],
            recv_sem=recv_a.at[j - 1],
            device_id={"dev": lax.rem(me_d + j, n_dev)},
            device_id_type=MESH,
        )
        copy.start()
        gather.append(copy)
    for copy in gather:
        copy.wait_recv()
    tile_row = lax.broadcasted_iota(jnp.int32, (8, 128), 0)
    tiles = []
    for d in range(n_dev):
        star_total = part_ref[0, d]
        for g in range(1, n_dev):
            star_total = star_total + part_ref[g, d]
        mass = jnp.where(tile_row < 4, star_total[0:1], star_total[4:5])
        floor = jnp.maximum(mass, 1.0)
        location = part_ref[d, n_dev]
        offset = (star_total - mass * location) / floor
        shift_ref[d] = offset
        tiles.append(
            jnp.where(lax.rem(tile_row, 4) == 0, 1.0 / floor, location + offset)
        )
    table = jnp.concatenate(tiles, axis=0)
    offset = shift_ref[me_d]
    for h in range(2):
        for c in range(2):
            offset_ref[c : c + 1, 128 * h : 128 * h + 128] = offset[
                4 * h + 1 + c : 4 * h + 2 + c
            ]
    table = jnp.concatenate(split3(table), axis=0)
    wide = jnp.zeros((MOMENTS, visits), F32)
    side = jnp.zeros((ROWS - MOMENTS, visits), F32)
    for basis, visit_hot, low_hot, predicted, weight, here in kept:
        found = three(dot(table, low_hot, NN), 8 * n_dev)
        chosen = jnp.where(here == 0, found[0:8], 0.0)
        for d in range(1, n_dev):
            chosen = chosen + jnp.where(here == 2 * d, found[8 * d : 8 * d + 8], 0.0)
        chosen = chosen[0:4] + chosen[4:8]
        normal = weight * (1.0 - weight * chosen[0:1])
        error = [weight * (predicted[c] - chosen[1 + c : 2 + c]) for c in range(2)]
        stack = []
        for a in range(13):
            stack += [normal * basis(a, group) for group in range(2 if a <= 4 else 1)]
        pieces = split3(jnp.concatenate(stack, axis=0))[:2]
        stack = []
        for c in range(2):
            stack += [error[c] * basis(a, 0) for a in range(7)]
        pieces += split3(jnp.concatenate(stack, axis=0))
        both = dot(jnp.concatenate(pieces, axis=0), visit_hot, NT)
        wide = wide + both[:MOMENTS] + both[MOMENTS : 2 * MOMENTS]
        side = side + three(both[2 * MOMENTS :], ROWS - MOMENTS)
    moments = jnp.concatenate([wide, side], axis=0)
    line_ref[2 * HALF - 16 :, :] = jnp.zeros((16, visits), F32)
    for to, source, count in packing()[0]:
        line_ref[to : to + count, :] = moments[source : source + count]
    moment_ref[me_p] = jnp.concatenate([line_ref[:HALF, :], line_ref[HALF:, :]], axis=1)
    spread = []
    for j in range(1, n_patch):
        copy = pltpu.make_async_remote_copy(
            src_ref=moment_ref.at[me_p],
            dst_ref=moment_ref.at[me_p],
            send_sem=send_c.at[j - 1],
            recv_sem=recv_c.at[j - 1],
            device_id={"patch": lax.rem(me_p + j, n_patch)},
            device_id_type=MESH,
        )
        copy.start()
        spread.append(copy)
    for copy in spread:
        copy.wait_recv()
    total = moment_ref[0]
    for p in range(1, n_patch):
        total = total + moment_ref[p]
    total_ref[...] = total
    for copy in gather + spread:
        copy.wait_send()


def per_device(n_dev, n_patch, plane, weight, visit, holder, star, coef, loc):
    rows = weight.shape[0]
    visits = coef.shape[0]
    scale = visits / (rows * n_patch)
    vmem = pl.BlockSpec(memory_space=pltpu.VMEM)
    dma = pltpu.SemaphoreType.DMA
    args = (
        plane,
        weight.reshape(1, rows),
        visit.reshape(1, rows),
        holder.reshape(1, rows),
        star.reshape(1, rows),
        coef.T,
        loc,
        jnp.asarray(coefficient_spread()),
        jnp.asarray(expansion()),
    )
    final = (
        jax.ShapeDtypeStruct((visits, NMON * NMON), F32),
        jax.ShapeDtypeStruct((2 * NMON, visits), F32),
        jax.ShapeDtypeStruct(loc.shape, F32),
    )
    first = (jax.ShapeDtypeStruct((HALF, 128), F32), final[2])
    outs = pl.pallas_call(
        functools.partial(kernel, n_dev, n_patch),
        out_shape=first,
        in_specs=[pl.BlockSpec(memory_space=pltpu.HBM)] * 8,
        out_specs=(vmem,) * len(first),
        scratch_shapes=[pltpu.VMEM(x.shape, x.dtype) for x in args[:8]]
        + [
            pltpu.VMEM((16, rows), F32),
            pltpu.VMEM((16, rows), F32),
            pltpu.VMEM((8, 128), F32),
            pltpu.VMEM((n_dev, n_dev + 1, 8, 128), F32),
            pltpu.VMEM((n_dev, 8, 128), F32),
            pltpu.VMEM((2 * HALF, visits), F32),
            pltpu.VMEM((n_patch, HALF, 128), F32),
            dma((8,)),
        ]
        + [dma((n_dev - 1,))] * 2
        + [dma((n_patch - 1,))] * 2,
        compiler_params=pltpu.CompilerParams(
            collective_id=0, has_side_effects=True, vmem_limit_bytes=62 * 1024 * 1024
        ),
    )(*args[:8])
    outs = pl.pallas_call(
        functools.partial(expand_kernel, scale, visits),
        out_shape=final,
        in_specs=[pl.BlockSpec(memory_space=pltpu.HBM)] * 3,
        out_specs=(vmem, vmem, pl.BlockSpec(memory_space=pltpu.HBM)),
        scratch_shapes=[
            pltpu.VMEM((HALF, 128), F32),
            pltpu.VMEM((ROWS, COLS), BF16),
            dma((3,)),
        ],
        compiler_params=pltpu.CompilerParams(vmem_limit_bytes=62 * 1024 * 1024),
    )(outs[0], outs[1], args[8])
    return outs[0], outs[1].T, outs[2]


def solution(mesh):
    placed = (
        P(None, ("patch", "dev")),
        P(("patch", "dev")),
        P(("patch", "dev")),
        P(("patch", "dev"), None),
        P(("patch", "dev")),
        P("dev", None),
        P(None, ("patch", "dev")),
    )
    return jax.shard_map(
        functools.partial(per_device, mesh.shape["dev"], mesh.shape["patch"]),
        mesh=mesh,
        in_specs=placed,
        out_specs=(P("dev", None), P("dev", None), P(None, ("patch", "dev"))),
        check_vma=False,
    )
```

```python
import functools
import math

import jax
import jax.numpy as jnp
import ml_dtypes
import numpy as np
from jax import lax
from jax.experimental import pallas as pl
from jax.experimental.pallas import tpu as pltpu
from jax.sharding import PartitionSpec as P

NMON = 28
DEG = 6
PAIRS = [(a, b) for a in range(DEG + 1) for b in range(DEG + 1 - a)]
MOMENTS = 144
ROWS = 256
COLS = 1024
RHS_COL = 896
F32 = jnp.float32
BF16 = jnp.bfloat16
MESH = pl.DeviceIdType.MESH
CHUNK = 2048
NT = (((1,), (1,)), ((), ()))
NN = (((1,), (0,)), ((), ()))


def moment_row(p, q):
    return 16 * p + q if p <= 4 else 80 + 8 * (p - 5) + q


HALF = 80


def packing():
    runs, end = [], 0
    for p in range(13):
        runs.append((end, moment_row(p, 0), 13 - p))
        end += 13 - p
    for c in range(2):
        for a in range(DEG + 1):
            runs.append((end, MOMENTS + c * 56 + a * 8, DEG + 1 - a))
            end += DEG + 1 - a
    return runs, end


def expansion():
    place = np.zeros((ROWS,), np.int32)
    for to, source, count in packing()[0]:
        for i in range(count):
            row = to + i
            place[source + i] = row if row < HALF else 128 + row - HALF
    table = np.zeros((ROWS, COLS), np.float32)
    for k, (a, b) in enumerate(PAIRS):
        for l, (c, d) in enumerate(PAIRS):
            for p in (a + c, abs(a - c)):
                for q in (b + d, abs(b - d)):
                    table[place[moment_row(p, q)], k * NMON + l] += 0.25
        for c in range(2):
            table[place[MOMENTS + c * 56 + a * 8 + b], RHS_COL + c * NMON + k] = 1.0
    return table.astype(ml_dtypes.bfloat16)


def coefficient_spread():
    table = np.zeros((112, 2 * NMON), np.float32)
    for k, (a, b) in enumerate(PAIRS):
        for c in range(2):
            table[c * 56 + a * 8 + b, c * NMON + k] = 1.0
    return table.astype(ml_dtypes.bfloat16)


def split3(x):
    high = x.astype(BF16)
    rest = x - high.astype(F32)
    middle = rest.astype(BF16)
    return high, middle, (rest - middle.astype(F32)).astype(BF16)


def dot(a, b, dims):
    return lax.dot_general(a, b, dims, preferred_element_type=F32)


def three(total, rows):
    return total[:rows] + total[rows : 2 * rows] + total[2 * rows : 3 * rows]


def widen(scale, visits, packed, expand_ref, blocks_ref, rhs_ref):
    turned = jnp.concatenate([packed, jnp.zeros((128 - HALF, 128), F32)], axis=0).T
    joined = jnp.concatenate([turned[:visits], turned[visits:]], axis=1)
    result = three(dot(jnp.concatenate(split3(joined), axis=0), expand_ref[...], NN), visits)
    blocks_ref[...] = result[:, : NMON * NMON] * scale
    ends = jnp.concatenate([result[:, RHS_COL:]] * 2, axis=0).T
    rhs_ref[...] = ends[: 2 * NMON, :visits] * math.sqrt(scale)


def expand_kernel(
    scale,
    visits,
    total_hbm,
    offset_hbm,
    expand_hbm,
    blocks_ref,
    rhs_ref,
    offset_out,
    total_ref,
    expand_ref,
    sems,
):
    copies = [
        pltpu.make_async_copy(source, target, sems.at[i])
        for i, (source, target) in enumerate(
            ((total_hbm, total_ref), (expand_hbm, expand_ref), (offset_hbm, offset_out))
        )
    ]
    for copy in copies:
        copy.start()
    for copy in copies[:2]:
        copy.wait()
    widen(scale, visits, total_ref[...], expand_ref, blocks_ref, rhs_ref)
    copies[2].wait()


def kernel(n_dev, n_patch, *refs):
    sources, refs = refs[:8], refs[8:]
    (total_ref, offset_ref), refs = refs[:2], refs[2:]
    held, refs = refs[:8], refs[8:]
    plane_ref, weight_ref, visit_ref, holder_ref, star_ref, coef_ref, loc_ref, spread_ref = held
    tu_ref, tv_ref, part_ref, shift_ref, line_ref, moment_ref, load_sem = refs[:7]
    send_a, recv_a, send_c, recv_c = refs[7:]
    loads = [
        pltpu.make_async_copy(source, target, load_sem.at[i])
        for i, (source, target) in enumerate(zip(sources, held))
    ]
    for load in loads:
        load.start()
    me_d = lax.axis_index("dev")
    me_p = lax.axis_index("patch")
    barrier = pltpu.get_barrier_semaphore()
    for j in range(1, n_dev):
        pl.semaphore_signal(
            barrier, inc=1, device_id={"dev": lax.rem(me_d + j, n_dev)}, device_id_type=MESH
        )
    for j in range(1, n_patch):
        pl.semaphore_signal(
            barrier, inc=1, device_id={"patch": lax.rem(me_p + j, n_patch)}, device_id_type=MESH
        )
    for load in loads:
        load.wait()

    rows = weight_ref.shape[1]
    visits = coef_ref.shape[1]
    weight = weight_ref[...]
    coords = plane_ref[...]
    series = [jnp.ones_like(coords), coords]
    for degree in range(2, 13):
        series.append(2.0 * coords * series[-1] - series[-2])
    tv_ref[...] = jnp.zeros_like(tv_ref)
    for degree, value in enumerate(series):
        tu_ref[degree : degree + 1, :] = value[0:1]
        tv_ref[degree : degree + 1, :] = value[1:2]

    coef = jnp.concatenate(
        [dot(spread_ref[...], piece, NN) for piece in split3(coef_ref[...])], axis=0
    ).astype(BF16)
    width = min(CHUNK, rows)
    sub = lax.broadcasted_iota(jnp.int32, (8, width), 0)
    half = lax.div(sub, 4)
    kind = lax.rem(sub, 4)
    sums = jnp.zeros((8 * n_dev, 128), F32)
    kept = []
    for start in range(0, rows, width):
        at = slice(start, start + width)

        def basis(a, group, at=at):
            return tu_ref[a : a + 1, at] * tv_ref[8 * group : 8 * group + 8, at]

        visit_hot = jnp.where(
            lax.broadcasted_iota(jnp.int32, (visits, width), 0) == visit_ref[:, at], 1.0, 0.0
        ).astype(BF16)
        picked = three(dot(coef, visit_hot, NN), 112)
        predicted = []
        for c in range(2):
            total = picked[c * 56 : c * 56 + 8] * basis(0, 0)
            for a in range(1, 7):
                total = total + picked[c * 56 + 8 * a : c * 56 + 8 * a + 8] * basis(a, 0)
            predicted.append(jnp.sum(total, axis=0, keepdims=True))
        star = star_ref[:, at]
        weight = weight_ref[:, at]
        place = holder_ref[:, at] * 2 + lax.div(star, 128)
        low_hot = jnp.where(
            lax.broadcasted_iota(jnp.int32, (128, width), 0) == lax.rem(star, 128), 1.0, 0.0
        ).astype(BF16)
        values = jnp.where(
            kind == 0,
            weight,
            jnp.where(
                kind == 1,
                weight * predicted[0],
                jnp.where(kind == 2, weight * predicted[1], 0.0),
            ),
        )
        here = place - half
        masked = []
        for piece in split3(values):
            piece = piece.astype(F32)
            masked += [jnp.where(here == 2 * d, piece, 0.0) for d in range(n_dev)]
        sums = sums + three(
            dot(jnp.concatenate(masked, axis=0).astype(BF16), low_hot, NT), 8 * n_dev
        )
        kept.append((basis, visit_hot, low_hot, predicted, weight, here))
    for d in range(n_dev):
        part_ref[me_d, d] = sums[8 * d : 8 * d + 8]
    for h in range(2):
        for c in range(2):
            part_ref[me_d, 2 * h + c, 3:4, :] = loc_ref[c : c + 1, 128 * h : 128 * h + 128]

    pl.semaphore_wait(barrier, n_dev + n_patch - 2)
    gather = []
    for j in range(1, n_dev):
        copy = pltpu.make_async_remote_copy(
            src_ref=part_ref.at[me_d],
            dst_ref=part_ref.at[me_d],
            send_sem=send_a.at[j - 1],
            recv_sem=recv_a.at[j - 1],
            device_id={"dev": lax.rem(me_d + j, n_dev)},
            device_id_type=MESH,
        )
        copy.start()
        gather.append(copy)
    for copy in gather:
        copy.wait_recv()
    tile_row = lax.broadcasted_iota(jnp.int32, (8, 128), 0)
    tiles = []
    none = jnp.zeros((1, 128), F32)
    for d in range(n_dev):
        star_total = part_ref[0, d]
        for g in range(1, n_dev):
            star_total = star_total + part_ref[g, d]
        mass = jnp.where(tile_row < 4, star_total[0:1], star_total[4:5])
        floor = jnp.maximum(mass, 1.0)
        near = [part_ref[d, r, 3:4, :] for r in range(4)]
        location = jnp.concatenate([none, *near[:2], none, none, *near[2:], none], axis=0)
        offset = (star_total - mass * location) / floor
        shift_ref[d] = offset
        tiles.append(
            jnp.where(lax.rem(tile_row, 4) == 0, 1.0 / floor, location + offset)
        )
    table = jnp.concatenate(tiles, axis=0)
    offset = shift_ref[me_d]
    for h in range(2):
        for c in range(2):
            offset_ref[c : c + 1, 128 * h : 128 * h + 128] = offset[
                4 * h + 1 + c : 4 * h + 2 + c
            ]
    table = jnp.concatenate(split3(table), axis=0)
    wide = jnp.zeros((MOMENTS, visits), F32)
    side = jnp.zeros((ROWS - MOMENTS, visits), F32)
    for basis, visit_hot, low_hot, predicted, weight, here in kept:
        found = three(dot(table, low_hot, NN), 8 * n_dev)
        chosen = jnp.where(here == 0, found[0:8], 0.0)
        for d in range(1, n_dev):
            chosen = chosen + jnp.where(here == 2 * d, found[8 * d : 8 * d + 8], 0.0)
        chosen = chosen[0:4] + chosen[4:8]
        normal = weight * (1.0 - weight * chosen[0:1])
        error = [weight * (predicted[c] - chosen[1 + c : 2 + c]) for c in range(2)]
        stack = []
        for a in range(13):
            stack += [normal * basis(a, group) for group in range(2 if a <= 4 else 1)]
        pieces = split3(jnp.concatenate(stack, axis=0))[:2]
        stack = []
        for c in range(2):
            stack += [error[c] * basis(a, 0) for a in range(7)]
        pieces += split3(jnp.concatenate(stack, axis=0))
        both = dot(jnp.concatenate(pieces, axis=0), visit_hot, NT)
        wide = wide + both[:MOMENTS] + both[MOMENTS : 2 * MOMENTS]
        side = side + three(both[2 * MOMENTS :], ROWS - MOMENTS)
    moments = jnp.concatenate([wide, side], axis=0)
    line_ref[2 * HALF - 16 :, :] = jnp.zeros((16, visits), F32)
    for to, source, count in packing()[0]:
        line_ref[to : to + count, :] = moments[source : source + count]
    moment_ref[me_p] = jnp.concatenate([line_ref[:HALF, :], line_ref[HALF:, :]], axis=1)
    spread = []
    for j in range(1, n_patch):
        copy = pltpu.make_async_remote_copy(
            src_ref=moment_ref.at[me_p],
            dst_ref=moment_ref.at[me_p],
            send_sem=send_c.at[j - 1],
            recv_sem=recv_c.at[j - 1],
            device_id={"patch": lax.rem(me_p + j, n_patch)},
            device_id_type=MESH,
        )
        copy.start()
        spread.append(copy)
    for copy in spread:
        copy.wait_recv()
    total = moment_ref[0]
    for p in range(1, n_patch):
        total = total + moment_ref[p]
    total_ref[...] = total
    for copy in gather + spread:
        copy.wait_send()


def per_device(n_dev, n_patch, plane, weight, visit, holder, star, coef, loc):
    rows = weight.shape[0]
    visits = coef.shape[0]
    scale = visits / (rows * n_patch)
    vmem = pl.BlockSpec(memory_space=pltpu.VMEM)
    dma = pltpu.SemaphoreType.DMA
    args = (
        plane,
        weight.reshape(1, rows),
        visit.reshape(1, rows),
        holder.reshape(1, rows),
        star.reshape(1, rows),
        coef.T,
        loc,
        jnp.asarray(coefficient_spread()),
        jnp.asarray(expansion()),
    )
    final = (
        jax.ShapeDtypeStruct((visits, NMON * NMON), F32),
        jax.ShapeDtypeStruct((2 * NMON, visits), F32),
        jax.ShapeDtypeStruct(loc.shape, F32),
    )
    first = (jax.ShapeDtypeStruct((HALF, 128), F32), final[2])
    outs = pl.pallas_call(
        functools.partial(kernel, n_dev, n_patch),
        out_shape=first,
        in_specs=[pl.BlockSpec(memory_space=pltpu.HBM)] * 8,
        out_specs=(vmem,) * len(first),
        scratch_shapes=[pltpu.VMEM(x.shape, x.dtype) for x in args[:8]]
        + [
            pltpu.VMEM((16, rows), F32),
            pltpu.VMEM((16, rows), F32),
            pltpu.VMEM((n_dev, n_dev, 8, 128), F32),
            pltpu.VMEM((n_dev, 8, 128), F32),
            pltpu.VMEM((2 * HALF, visits), F32),
            pltpu.VMEM((n_patch, HALF, 128), F32),
            dma((8,)),
        ]
        + [dma((n_dev - 1,))] * 2
        + [dma((n_patch - 1,))] * 2,
        compiler_params=pltpu.CompilerParams(
            collective_id=0, has_side_effects=True, vmem_limit_bytes=62 * 1024 * 1024
        ),
    )(*args[:8])
    outs = pl.pallas_call(
        functools.partial(expand_kernel, scale, visits),
        out_shape=final,
        in_specs=[pl.BlockSpec(memory_space=pltpu.HBM)] * 3,
        out_specs=(vmem, vmem, pl.BlockSpec(memory_space=pltpu.HBM)),
        scratch_shapes=[
            pltpu.VMEM((HALF, 128), F32),
            pltpu.VMEM((ROWS, COLS), BF16),
            dma((3,)),
        ],
        compiler_params=pltpu.CompilerParams(vmem_limit_bytes=62 * 1024 * 1024),
    )(outs[0], outs[1], args[8])
    return outs[0], outs[1].T, outs[2]


def solution(mesh):
    placed = (
        P(None, ("patch", "dev")),
        P(("patch", "dev")),
        P(("patch", "dev")),
        P(("patch", "dev"), None),
        P(("patch", "dev")),
        P("dev", None),
        P(None, ("patch", "dev")),
    )
    return jax.shard_map(
        functools.partial(per_device, mesh.shape["dev"], mesh.shape["patch"]),
        mesh=mesh,
        in_specs=placed,
        out_specs=(P("dev", None), P("dev", None), P(None, ("patch", "dev"))),
        check_vma=False,
    )
```
